32 devices in a mesh: groups: 2 (over y), seq: 4 (over z), chan: 4 (over x, core).
Axes of the slice: x: 2, y: 2, z: 4, core: 2. Of those that a mesh axis runs over, the one named last changes fastest.
Arguments:
- value: bfloat16 [1024, 4096], P(('groups', 'seq'), 'chan'), parts along dimension 0, may hold values from -6 to 6
- first_gate: bfloat16 [1024, 4096], P(('groups', 'seq'), 'chan'), parts along dimension 0, may hold values from -6 to 6
- second_gate: bfloat16 [1024, 4096], P(('groups', 'seq'), 'chan'), parts along dimension 0, may hold values from -6 to 6
- first_filter: bfloat16 [256, 512], P('chan'), may hold values from -0.25 to 0.25
- second_filter: bfloat16 [256, 512], P('chan'), may hold values from -0.25 to 0.25
- out_weight: bfloat16 [4096, 4096], P('chan'), may hold values from -0.09375 to 0.09375
- segment_ids: int32 [1024], P(('groups', 'seq')), parts along dimension 0, may hold values from 0 to 1, never falling along the last dimension, each value on 1 to 384 neighbouring positions
Outputs:
- mixed: bfloat16 [1024, 4096], P(('groups', 'seq')), parts along dimension 0
The draws below stay inside these ranges and needn't reach their ends.
There are 2 independent parts, one for each index of `groups`. The reference program is written for one: setup_inputs(seed, part) draws one part's arguments, and reference() takes and returns one part's arrays. A program takes and returns all parts, laid end to end along the dimension named above; an argument that names none is the same for every part. Nothing has to cross between parts.
Inputs may be any that keep to these rules, and one draw needn't show every extreme that they name: `segment_ids`: ids never fall along the window; the 2 contexts each hold 128 to 384 neighbouring positions and together fill the window.
All inputs are finite; a program needn't handle non-finite values.
Results may differ from the reference program's by a relative error of at most 0.0065.
Values may be sent and summed in bfloat16 or wider, within the bound.
A program may use at most 192 MiB of HBM per device.

```python
import math
import jax
import jax.numpy as jnp
import numpy as np

D = 4096
FILT_GROUP = 16
FILTERS = 256
SEQ_LEN = 512
SEGMENTS = 2
MOST = 384


def steps_of(key, dims, shards, least, largest):
    loudness = 1.0
    for position, blocks in shards:
        draws = jax.random.uniform(jax.random.fold_in(jax.random.fold_in(key, 6), position), (blocks,), jnp.float32, least / len(shards), largest / len(shards))
        loudness = loudness * jnp.repeat(jnp.exp(draws), dims[position] // blocks).reshape((-1,) + (1,) * (len(dims) - 1 - position))
    return loudness


def profile(amount, total, most, skew):
    weights = [(1 << 20) // math.isqrt(standing ** skew) + 1 for standing in range(2, amount + 1)]
    surplus, holding = total - most - (amount - 1), [1] * (amount - 1)
    while surplus > 0:
        free = [i for i in range(amount - 1) if holding[i] < most]
        pool, budget = sum([weights[i] for i in free]), surplus
        for i in free:
            more = min(most - holding[i], max(1, budget * weights[i] // pool), surplus)
            holding[i] = holding[i] + more
            surplus = surplus - more
    return np.array([most] + holding)


def uneven(key, count, total, most, lean):
    if count == 2:
        one = jax.random.randint(key, (), max(1, total - most), min(most, total - 1) + 1)
        return jnp.stack([one, total - one])
    lengths = jnp.asarray(profile(count, total, most, lean), jnp.int32)
    twos = (count - 1) // 2
    source_of, taker = lengths[1:1 + 2 * twos:2], lengths[2:2 + 2 * twos:2]
    slack = jnp.minimum(source_of - 1, most - taker)
    shifted = jax.random.randint(jax.random.fold_in(key, 1), (twos,), 0, 1 << 20) % (slack + 1)
    lengths = lengths.at[1:1 + 2 * twos:2].set(source_of - shifted).at[2:2 + 2 * twos:2].set(taker + shifted)
    return lengths[jax.random.permutation(jax.random.fold_in(key, 2), count)]


def gaussian(own_key, shape, scale, bound, split=(), dtype=jnp.bfloat16):
    result = scale * jax.random.normal(own_key, shape, jnp.float32)
    if split:
        result = result * steps_of(own_key, shape, split, -0.22, 0.18)
    return jnp.clip(result, -bound, bound).astype(dtype)


def setup_inputs(seed: int = 0, part: int = 0) -> dict:
    seeds = jax.random.split(jax.random.key(seed), 8)
    own_keys = jax.random.split(jax.random.fold_in(seeds[7], part), 8)
    value = gaussian(own_keys[0], (SEQ_LEN, D), 1.0, 6.0, ((0, 4), (1, 4)))
    first_gate = gaussian(own_keys[1], (SEQ_LEN, D), 1.0, 6.0, ((0, 4), (1, 4)))
    second_gate = gaussian(own_keys[2], (SEQ_LEN, D), 1.0, 6.0, ((0, 4), (1, 4)))
    first_filter = gaussian(seeds[3], (FILTERS, SEQ_LEN), SEQ_LEN ** -0.5, 0.25, ((0, 4),))
    second_filter = gaussian(seeds[4], (FILTERS, SEQ_LEN), SEQ_LEN ** -0.5, 0.25, ((0, 4),))
    out_weight = gaussian(seeds[5], (D, D), D ** -0.5, 0.09375, ((0, 4),))
    segment_ids = jnp.searchsorted(jnp.cumsum(uneven(own_keys[6], SEGMENTS, SEQ_LEN, MOST, 0)), jnp.arange(SEQ_LEN), side="right").astype(jnp.int32)
    return dict(value=value, first_gate=first_gate, second_gate=second_gate, first_filter=first_filter, second_filter=second_filter, out_weight=out_weight, segment_ids=segment_ids)


def long_conv(filters, field, segment_ids):
    length, width = field.shape
    spectrum = jnp.fft.rfft(filters.astype(jnp.float32), axis=1)
    spectrum = jnp.repeat(spectrum, FILT_GROUP, axis=0).T
    total = jnp.zeros((length, width), jnp.float32)
    for which in range(SEGMENTS):
        inside = (segment_ids == which).astype(jnp.float32)[:, None]
        masked = field.astype(jnp.float32) * inside
        mixed_part = jnp.fft.irfft(jnp.fft.rfft(masked, axis=0) * spectrum, n=length, axis=0)
        total = total + mixed_part.astype(jnp.float32) * inside
    return total


def reference(value, first_gate, second_gate, first_filter, second_filter, out_weight, segment_ids):
    first_input = (first_gate.astype(jnp.float32) * value.astype(jnp.float32)).astype(jnp.bfloat16)
    first_mix = long_conv(first_filter, first_input, segment_ids)
    second_input = (second_gate.astype(jnp.float32) * first_mix).astype(jnp.bfloat16)
    second_mix = long_conv(second_filter, second_input, segment_ids).astype(jnp.bfloat16)
    return jnp.dot(second_mix, out_weight, preferred_element_type=jnp.float32).astype(jnp.bfloat16)
```

```python
import functools

import jax
import jax.numpy as jnp
from jax import lax
from jax.experimental import pallas as pl
from jax.experimental.pallas import tpu as pltpu
from jax.sharding import PartitionSpec as P

MESH = pl.DeviceIdType.MESH
TILE = 256
LANES = 128
CORES = 2


def remote(src, dst, send, recv, where):
    return pltpu.make_async_remote_copy(
        src_ref=src, dst_ref=dst, send_sem=send, recv_sem=recv, device_id=where, device_id_type=MESH
    )


def kernel(
    seqs, chans, chunks,
    value, gate1, gate2, filt1, filt2, weight, segs,
    out,
    taps_f32, taps, z_send, z_recv, g_send, g_recv, seg_all, mix, m_send, m_recv,
    w_buf, p_send, p_recv, x_buf,
    w_sem, z_ss, z_rs, g_ss, g_rs, s_ss, s_rs, m_ss, m_rs, p_ss, p_rs, x_ss, x_rs, o_ss, o_rs,
):
    me = lax.axis_index("seq")
    chan = lax.axis_index("chan")
    chips = chans // CORES
    core = lax.rem(chan, CORES)
    chip = lax.div(chan, CORES)
    partner = chip * CORES + (1 - core)
    tok = value.shape[0]
    length = filt1.shape[1]
    mine_filts = taps.shape[1]
    rows = z_send.shape[1]
    per = rows // mine_filts
    blocks = length // TILE
    half_cols = weight.shape[1] // CORES
    width = half_cols // chunks

    seq_peers = [lax.rem(me + d, seqs) for d in range(1, seqs)]
    chip_peers = [lax.rem(chip + d, chips) * CORES + core for d in range(1, chips)]

    barrier = pltpu.get_barrier_semaphore()
    for peer in seq_peers:
        pl.semaphore_signal(barrier, inc=1, device_id={"seq": peer}, device_id_type=MESH)
    for peer in chip_peers + [partner]:
        pl.semaphore_signal(barrier, inc=1, device_id={"chan": peer}, device_id_type=MESH)

    w_copies = []
    for side in range(CORES):
        owner = 1 - core if side == 0 else core
        for q in range(chunks):
            at = pl.multiple_of(owner * half_cols + q * width, width)
            copy = pltpu.make_async_copy(
                weight.at[:, pl.ds(at, width)], w_buf.at[side, q], w_sem.at[side, q]
            )
            copy.start()
            w_copies.append(copy)

    prod = (gate1[...].astype(jnp.float32) * value[...].astype(jnp.float32)).astype(jnp.bfloat16)
    z_send[...] = prod.T.reshape(seqs, rows, tok)

    pl.semaphore_wait(barrier, seqs - 1 + chips)

    copies = []
    for d, peer in enumerate(seq_peers):
        copy = remote(segs, seg_all.at[me], s_ss.at[d], s_rs.at[d], {"seq": peer})
        copy.start()
        copies.append(copy)
    for d, peer in enumerate(seq_peers):
        copy = remote(z_send.at[peer], z_recv.at[me], z_ss.at[d], z_rs.at[d], {"seq": peer})
        copy.start()
        copies.append(copy)
    g_send[...] = gate2[...].T.reshape(seqs, rows, tok)
    g_copies = []
    for d, peer in enumerate(seq_peers):
        copy = remote(g_send.at[peer], g_recv.at[me], g_ss.at[d], g_rs.at[d], {"seq": peer})
        copy.start()
        g_copies.append(copy)
    seg_all[me] = segs[...]
    z_recv[me] = z_send[me]
    g_recv[me] = g_send[me]

    for which, filt in enumerate((filt1, filt2)):
        taps_f32[which] = filt[...].astype(jnp.float32)

        def build(f, carry):
            row = taps_f32[which, pl.ds(me * mine_filts + f, 1), :]
            wide = jnp.broadcast_to(row, (LANES, length))
            low = pltpu.roll(wide, 0, 1, stride=1, stride_axis=0).astype(jnp.bfloat16)
            taps[which, f, pl.ds(0, LANES), :] = low
            taps[which, f, pl.ds(LANES, LANES), :] = jnp.concatenate(
                [low[:, length - LANES :], low[:, : length - LANES]], axis=1
            )
            return carry

        lax.fori_loop(0, mine_filts, build, 0)

    for copy in copies:
        copy.wait_recv()

    ids = jnp.concatenate([seg_all[j] for j in range(seqs)], axis=1)
    first = jnp.broadcast_to((ids == 0).astype(jnp.float32), (per, length))
    in_first = first > 0.5
    keep = (first.astype(jnp.bfloat16), (1.0 - first).astype(jnp.bfloat16))

    def conv(which, f, field):
        parts = []
        for j in range(blocks):
            span = slice(j * TILE, (j + 1) * TILE)
            parts += [field[:, span] * keep[0][:, span], field[:, span] * keep[1][:, span]]
        lhs = jnp.concatenate(parts, axis=0)
        res = jnp.dot(lhs, taps[which, f], preferred_element_type=jnp.float32)
        sums = []
        for context in range(2):
            total = None
            for j in range(blocks):
                at = (2 * j + context) * per
                piece = res[at : at + per]
                if j:
                    cut = length - j * TILE
                    piece = jnp.concatenate([piece[:, cut:], piece[:, :cut]], axis=1)
                total = piece if total is None else total + piece
            sums.append(total)
        return jnp.where(in_first, sums[0], sums[1])

    def rows_of(f):
        return pl.ds(pl.multiple_of(f * per, per), per)

    def first_conv(f, carry):
        field = jnp.concatenate([z_recv[j, rows_of(f), :] for j in range(seqs)], axis=1)
        mix[rows_of(f), :] = conv(0, f, field)
        return carry

    lax.fori_loop(0, mine_filts, first_conv, 0)

    for copy in g_copies:
        copy.wait_recv()

    def second_conv(f, carry):
        gate = jnp.concatenate([g_recv[j, rows_of(f), :] for j in range(seqs)], axis=1)
        field = (gate.astype(jnp.float32) * mix[rows_of(f), :]).astype(jnp.bfloat16)
        result = conv(1, f, field).astype(jnp.bfloat16)
        for j in range(seqs):
            m_send[j, rows_of(f), :] = result[:, j * tok : (j + 1) * tok]
        return carry

    lax.fori_loop(0, mine_filts, second_conv, 0)

    m_copies = []
    for d, peer in enumerate(seq_peers):
        copy = remote(m_send.at[peer], m_recv.at[me], m_ss.at[d], m_rs.at[d], {"seq": peer})
        copy.start()
        m_copies.append(copy)
    m_recv[me] = m_send[me]
    for copy in w_copies:
        copy.wait()
    for copy in m_copies:
        copy.wait_recv()

    lhs = m_recv[...].reshape(seqs * rows, tok).T
    p_copies = []
    for q in range(chunks):
        p_send[q] = jnp.dot(lhs, w_buf[0, q], preferred_element_type=jnp.float32).astype(jnp.bfloat16)
        copy = remote(p_send.at[q], p_recv.at[q], p_ss.at[q], p_rs.at[q], {"chan": partner})
        copy.start()
        p_copies.append(copy)
    x_copies = []
    for q in range(chunks):
        part = jnp.dot(lhs, w_buf[1, q], preferred_element_type=jnp.float32)
        p_copies[q].wait_recv()
        x_buf[chip, q] = (part + p_recv[q].astype(jnp.float32)).astype(jnp.bfloat16)
        x_copies.append([])
        for d, peer in enumerate(chip_peers):
            copy = remote(x_buf.at[chip, q], x_buf.at[chip, q], x_ss.at[q, d], x_rs.at[q, d], {"chan": peer})
            copy.start()
            x_copies[q].append(copy)
    o_copies = []
    for q in range(chunks):
        for copy in x_copies[q]:
            copy.wait_recv()
        total = x_buf[0, q].astype(jnp.float32)
        for j in range(1, chips):
            total = total + x_buf[j, q].astype(jnp.float32)
        here = out.at[:, pl.ds(pl.multiple_of(core * half_cols + q * width, width), width)]
        here[...] = total.astype(jnp.bfloat16)
        copy = remote(here, here, o_ss.at[q], o_rs.at[q], {"chan": partner})
        copy.start()
        o_copies.append(copy)
    for copy in copies + g_copies + m_copies + p_copies + [c for cs in x_copies for c in cs]:
        copy.wait_send()
    for copy in o_copies:
        copy.wait()


def local(seqs, chans, value, gate1, gate2, filt1, filt2, weight, segs):
    tok, width = value.shape
    filts, length = filt1.shape
    cols = weight.shape[1]
    chips = chans // CORES
    chunks = 4
    chunk = cols // CORES // chunks
    mine = filts // seqs
    rows = width // seqs
    bf16, f32 = jnp.bfloat16, jnp.float32
    dma = pltpu.SemaphoreType.DMA
    others = seqs - 1
    vmem = pl.BlockSpec(memory_space=pltpu.VMEM)
    return pl.pallas_call(
        functools.partial(kernel, seqs, chans, chunks),
        out_shape=jax.ShapeDtypeStruct((tok, cols), bf16),
        in_specs=[vmem] * 5 + [pl.BlockSpec(memory_space=pl.ANY), vmem],
        out_specs=vmem,
        scratch_shapes=[
            pltpu.VMEM((2, filts, length), f32),
            pltpu.VMEM((2, mine, TILE, length), bf16),
            pltpu.VMEM((seqs, rows, tok), bf16),
            pltpu.VMEM((seqs, rows, tok), bf16),
            pltpu.VMEM((seqs, rows, tok), bf16),
            pltpu.VMEM((seqs, rows, tok), bf16),
            pltpu.VMEM((seqs, 1, tok), jnp.int32),
            pltpu.VMEM((rows, length), f32),
            pltpu.VMEM((seqs, rows, tok), bf16),
            pltpu.VMEM((seqs, rows, tok), bf16),
            pltpu.VMEM((CORES, chunks, width, chunk), bf16),
            pltpu.VMEM((chunks, tok, chunk), bf16),
            pltpu.VMEM((chunks, tok, chunk), bf16),
            pltpu.VMEM((chips, chunks, tok, chunk), bf16),
            dma((CORES, chunks)),
            dma((others,)), dma((others,)), dma((others,)), dma((others,)),
            dma((others,)), dma((others,)), dma((others,)), dma((others,)),
            dma((chunks,)), dma((chunks,)),
            dma((chunks, chips - 1)), dma((chunks, chips - 1)),
            dma((chunks,)), dma((chunks,)),
        ],
        compiler_params=pltpu.CompilerParams(
            collective_id=0, has_side_effects=True, vmem_limit_bytes=48 * 1024 * 1024
        ),
    )(value, gate1, gate2, filt1, filt2, weight, segs.reshape(1, tok))


def solution(mesh):
    in_specs = (
        P(("groups", "seq"), "chan"),
        P(("groups", "seq"), "chan"),
        P(("groups", "seq"), "chan"),
        P("chan", None),
        P("chan", None),
        P("chan", None),
        P(("groups", "seq")),
    )
    out_specs = P(("groups", "seq"), None)
    body = functools.partial(local, mesh.shape["seq"], mesh.shape["chan"])
    return jax.shard_map(body, mesh=mesh, in_specs=in_specs, out_specs=out_specs, check_vma=False)
```

```python
import functools
import math

import jax
import jax.numpy as jnp
from jax import lax
from jax.experimental import pallas as pl
from jax.experimental.pallas import tpu as pltpu
from jax.sharding import PartitionSpec as P

MESH = pl.DeviceIdType.MESH
TILE = 256
LANES = 128
CORES = 2
GROUP = 4
PARTS = 2


def remote(src, dst, send, recv, where):
    return pltpu.make_async_remote_copy(
        src_ref=src, dst_ref=dst, send_sem=send, recv_sem=recv, device_id=where, device_id_type=MESH
    )


def kernel(
    seqs, chans, chunks,
    value_in, gate1_in, gate2_in, filt1_in, filt2_in, weight, segs_in,
    out,
    value, gate1, gate2, filt1, filt2, segs,
    taps_f32, taps, z_send, z_recv, g_send, g_recv, seg_all, mix, m_send, m_recv,
    w_buf, p_send, p_recv, x_buf,
    i_sem, w_sem, z_ss, z_rs, g_ss, g_rs, s_ss, s_rs, m_ss, m_rs, p_ss, p_rs, x_ss, x_rs, o_ss, o_rs,
):
    me = lax.axis_index("seq")
    chan = lax.axis_index("chan")
    chips = chans // CORES
    core = lax.rem(chan, CORES)
    chip = lax.div(chan, CORES)
    partner = chip * CORES + (1 - core)
    tok = value.shape[0]
    length = filt1.shape[1]
    mine_filts = taps.shape[1]
    rows = z_send.shape[1]
    per = rows // mine_filts
    blocks = length // TILE
    parts = z_ss.shape[0]
    part_filts = mine_filts // parts
    part_rows = rows // parts
    step = math.gcd(part_filts, GROUP)
    half_cols = weight.shape[1] // CORES
    width = half_cols // chunks

    seq_peers = [lax.rem(me + d, seqs) for d in range(1, seqs)]
    chip_peers = [lax.rem(chip + d, chips) * CORES + core for d in range(1, chips)]

    barrier = pltpu.get_barrier_semaphore()
    for peer in seq_peers:
        pl.semaphore_signal(barrier, inc=1, device_id={"seq": peer}, device_id_type=MESH)
    for peer in chip_peers + [partner]:
        pl.semaphore_signal(barrier, inc=1, device_id={"chan": peer}, device_id_type=MESH)

    ins = []
    pairs = ((value_in, value), (gate1_in, gate1), (gate2_in, gate2), (filt1_in, filt1), (filt2_in, filt2), (segs_in, segs))
    for index, (source, target) in enumerate(pairs):
        copy = pltpu.make_async_copy(source, target, i_sem.at[index])
        copy.start()
        ins.append(copy)

    w_copies = []
    for side in range(CORES):
        owner = 1 - core if side == 0 else core
        for q in range(chunks):
            at = pl.multiple_of(owner * half_cols + q * width, width)
            copy = pltpu.make_async_copy(
                weight.at[:, pl.ds(at, width)], w_buf.at[side, q], w_sem.at[side, q]
            )
            copy.start()
            w_copies.append(copy)

    ins[0].wait()
    ins[1].wait()
    prod = (gate1[...].astype(jnp.float32) * value[...].astype(jnp.float32)).astype(jnp.bfloat16)
    z_send[...] = prod.T.reshape(seqs, rows, tok)

    pl.semaphore_wait(barrier, seqs - 1 + chips)

    def exchange(source, target, sends, recvs, part):
        span = pl.ds(part * part_rows, part_rows)
        started = []
        for d, peer in enumerate(seq_peers):
            copy = remote(
                source.at[peer, span], target.at[me, span], sends.at[part, d], recvs.at[part, d], {"seq": peer}
            )
            copy.start()
            started.append(copy)
        return started

    ins[5].wait()
    s_copies = []
    for d, peer in enumerate(seq_peers):
        copy = remote(segs, seg_all.at[me], s_ss.at[d], s_rs.at[d], {"seq": peer})
        copy.start()
        s_copies.append(copy)
    z_copies = [exchange(z_send, z_recv, z_ss, z_rs, 0)]
    ins[2].wait()
    g_send[...] = gate2[...].T.reshape(seqs, rows, tok)
    g_copies = [exchange(g_send, g_recv, g_ss, g_rs, 0)]
    for part in range(1, parts):
        z_copies.append(exchange(z_send, z_recv, z_ss, z_rs, part))
        g_copies.append(exchange(g_send, g_recv, g_ss, g_rs, part))
    seg_all[me] = segs[...]
    z_recv[me] = z_send[me]
    g_recv[me] = g_send[me]

    def build_taps(which, filt):
        taps_f32[which] = filt[...].astype(jnp.float32)

        def build(f, carry):
            row = taps_f32[which, pl.ds(me * mine_filts + f, 1), :]
            wide = jnp.broadcast_to(row, (LANES, length))
            low = pltpu.roll(wide, 0, 1, stride=1, stride_axis=0).astype(jnp.bfloat16)
            taps[which, f, pl.ds(0, LANES), :] = low
            taps[which, f, pl.ds(LANES, LANES), :] = jnp.concatenate(
                [low[:, length - LANES :], low[:, : length - LANES]], axis=1
            )
            return carry

        lax.fori_loop(0, mine_filts, build, 0)

    ins[3].wait()
    ins[4].wait()
    build_taps(0, filt1)

    for copy in s_copies:
        copy.wait_recv()

    ids = jnp.concatenate([seg_all[j] for j in range(seqs)], axis=1)
    first = jnp.broadcast_to((ids == 0).astype(jnp.float32), (per, length))
    in_first = first > 0.5
    keep = (first.astype(jnp.bfloat16), (1.0 - first).astype(jnp.bfloat16))

    def conv(which, f, field):
        parts = []
        for j in range(blocks):
            span = slice(j * TILE, (j + 1) * TILE)
            parts += [field[:, span] * keep[0][:, span], field[:, span] * keep[1][:, span]]
        lhs = jnp.concatenate(parts, axis=0)
        res = jnp.dot(lhs, taps[which, f], preferred_element_type=jnp.float32)
        sums = []
        for context in range(2):
            total = None
            for j in range(blocks):
                at = (2 * j + context) * per
                piece = res[at : at + per]
                if j:
                    cut = length - j * TILE
                    piece = jnp.concatenate([piece[:, cut:], piece[:, :cut]], axis=1)
                total = piece if total is None else total + piece
            sums.append(total)
        return jnp.where(in_first, sums[0], sums[1])

    def rows_of(f):
        return pl.ds(pl.multiple_of(f * per, per), per)

    def joined(ref, f):
        return jnp.concatenate([ref[j, rows_of(f), :] for j in range(seqs)], axis=1)

    def first_conv(base, i, carry):
        at = [base + i * step + k for k in range(step)]
        fields = [joined(z_recv, f) for f in at]
        results = [conv(0, f, field) for f, field in zip(at, fields)]
        for f, result in zip(at, results):
            mix[rows_of(f), :] = result
        return carry

    def second_conv(base, i, carry):
        at = [base + i * step + k for k in range(step)]
        fields = [(joined(g_recv, f).astype(jnp.float32) * mix[rows_of(f), :]).astype(jnp.bfloat16) for f in at]
        results = [conv(1, f, field).astype(jnp.bfloat16) for f, field in zip(at, fields)]
        for f, result in zip(at, results):
            for j in range(seqs):
                m_send[j, rows_of(f), :] = result[:, j * tok : (j + 1) * tok]
        return carry

    m_copies = []
    for part in range(parts):
        base = part * part_filts
        for copy in z_copies[part]:
            copy.wait_recv()
        lax.fori_loop(0, part_filts // step, functools.partial(first_conv, base), 0)
        if part == 0:
            build_taps(1, filt2)
        for copy in g_copies[part]:
            copy.wait_recv()
        lax.fori_loop(0, part_filts // step, functools.partial(second_conv, base), 0)
        m_copies += exchange(m_send, m_recv, m_ss, m_rs, part)
    m_recv[me] = m_send[me]
    for copy in w_copies:
        copy.wait()
    for copy in m_copies:
        copy.wait_recv()

    lhs = m_recv[...].reshape(seqs * rows, tok).T
    p_copies = []
    for q in range(chunks):
        p_send[q] = jnp.dot(lhs, w_buf[0, q], preferred_element_type=jnp.float32).astype(jnp.bfloat16)
        copy = remote(p_send.at[q], p_recv.at[q], p_ss.at[q], p_rs.at[q], {"chan": partner})
        copy.start()
        p_copies.append(copy)
    x_copies = []
    for q in range(chunks):
        part = jnp.dot(lhs, w_buf[1, q], preferred_element_type=jnp.float32)
        p_copies[q].wait_recv()
        x_buf[chip, q] = (part + p_recv[q].astype(jnp.float32)).astype(jnp.bfloat16)
        x_copies.append([])
        for d, peer in enumerate(chip_peers):
            copy = remote(x_buf.at[chip, q], x_buf.at[chip, q], x_ss.at[q, d], x_rs.at[q, d], {"chan": peer})
            copy.start()
            x_copies[q].append(copy)
    o_copies = []
    for q in range(chunks):
        for copy in x_copies[q]:
            copy.wait_recv()
        total = x_buf[0, q].astype(jnp.float32)
        for j in range(1, chips):
            total = total + x_buf[j, q].astype(jnp.float32)
        here = out.at[:, pl.ds(pl.multiple_of(core * half_cols + q * width, width), width)]
        here[...] = total.astype(jnp.bfloat16)
        copy = remote(here, here, o_ss.at[q], o_rs.at[q], {"chan": partner})
        copy.start()
        o_copies.append(copy)
    nested = [c for cs in z_copies + g_copies + x_copies for c in cs]
    for copy in s_copies + nested + m_copies + p_copies:
        copy.wait_send()
    for copy in o_copies:
        copy.wait()


def local(seqs, chans, value, gate1, gate2, filt1, filt2, weight, segs):
    tok, width = value.shape
    filts, length = filt1.shape
    cols = weight.shape[1]
    chips = chans // CORES
    chunks = 4
    chunk = cols // CORES // chunks
    mine = filts // seqs
    rows = width // seqs
    bf16, f32 = jnp.bfloat16, jnp.float32
    dma = pltpu.SemaphoreType.DMA
    others = seqs - 1
    parts = math.gcd(mine, PARTS)
    vmem = pl.BlockSpec(memory_space=pltpu.VMEM)
    return pl.pallas_call(
        functools.partial(kernel, seqs, chans, chunks),
        out_shape=jax.ShapeDtypeStruct((tok, cols), bf16),
        in_specs=[pl.BlockSpec(memory_space=pl.ANY)] * 7,
        out_specs=vmem,
        scratch_shapes=[
            pltpu.VMEM((tok, width), bf16),
            pltpu.VMEM((tok, width), bf16),
            pltpu.VMEM((tok, width), bf16),
            pltpu.VMEM((filts, length), bf16),
            pltpu.VMEM((filts, length), bf16),
            pltpu.VMEM((1, tok), jnp.int32),
            pltpu.VMEM((2, filts, length), f32),
            pltpu.VMEM((2, mine, TILE, length), bf16),
            pltpu.VMEM((seqs, rows, tok), bf16),
            pltpu.VMEM((seqs, rows, tok), bf16),
            pltpu.VMEM((seqs, rows, tok), bf16),
            pltpu.VMEM((seqs, rows, tok), bf16),
            pltpu.VMEM((seqs, 1, tok), jnp.int32),
            pltpu.VMEM((rows, length), f32),
            pltpu.VMEM((seqs, rows, tok), bf16),
            pltpu.VMEM((seqs, rows, tok), bf16),
            pltpu.VMEM((CORES, chunks, width, chunk), bf16),
            pltpu.VMEM((chunks, tok, chunk), bf16),
            pltpu.VMEM((chunks, tok, chunk), bf16),
            pltpu.VMEM((chips, chunks, tok, chunk), bf16),
            dma((6,)),
            dma((CORES, chunks)),
            dma((parts, others)), dma((parts, others)), dma((parts, others)), dma((parts, others)),
            dma((others,)), dma((others,)), dma((parts, others)), dma((parts, others)),
            dma((chunks,)), dma((chunks,)),
            dma((chunks, chips - 1)), dma((chunks, chips - 1)),
            dma((chunks,)), dma((chunks,)),
        ],
        compiler_params=pltpu.CompilerParams(
            collective_id=0, has_side_effects=True, vmem_limit_bytes=58 * 1024 * 1024
        ),
    )(value, gate1, gate2, filt1, filt2, weight, segs.reshape(1, tok))


def solution(mesh):
    in_specs = (
        P(("groups", "seq"), "chan"),
        P(("groups", "seq"), "chan"),
        P(("groups", "seq"), "chan"),
        P("chan", None),
        P("chan", None),
        P("chan", None),
        P(("groups", "seq")),
    )
    out_specs = P(("groups", "seq"), None)
    body = functools.partial(local, mesh.shape["seq"], mesh.shape["chan"])
    return jax.shard_map(body, mesh=mesh, in_specs=in_specs, out_specs=out_specs, check_vma=False)
```

```python
import functools
import math

import jax
import jax.numpy as jnp
from jax import lax
from jax.experimental import pallas as pl
from jax.experimental.pallas import tpu as pltpu
from jax.sharding import PartitionSpec as P

MESH = pl.DeviceIdType.MESH
TILE = 256
LANES = 128
CORES = 2
GROUP = 4
PARTS = 2
HALVES = 2


def remote(src, dst, send, recv, where):
    return pltpu.make_async_remote_copy(
        src_ref=src, dst_ref=dst, send_sem=send, recv_sem=recv, device_id=where, device_id_type=MESH
    )


def kernel(
    seqs, chans, chunks,
    value_in, gate1_in, gate2_in, filt1_in, filt2_in, weight, segs_in,
    out,
    value, gate1, gate2, filt1, filt2, segs,
    taps_f32, taps, z_send, z_recv, g_send, g_recv, seg_all, mix, m_cols, m_send, m_recv,
    w_buf, p_send, p_recv, x_buf,
    i_sem, w_sem, z_ss, z_rs, g_ss, g_rs, s_ss, s_rs, m_ss, m_rs, p_ss, p_rs, x_ss, x_rs, o_ss, o_rs,
):
    me = lax.axis_index("seq")
    chan = lax.axis_index("chan")
    chips = chans // CORES
    core = lax.rem(chan, CORES)
    chip = lax.div(chan, CORES)
    partner = chip * CORES + (1 - core)
    tok = value.shape[0]
    length = filt1.shape[1]
    mine_filts = taps.shape[1]
    rows = z_send.shape[1]
    per = rows // mine_filts
    blocks = length // TILE
    parts = z_ss.shape[0]
    part_filts = mine_filts // parts
    part_rows = rows // parts
    step = math.gcd(part_filts, GROUP)
    half_cols = weight.shape[1] // CORES
    width = half_cols // chunks

    seq_peers = [lax.rem(me + d, seqs) for d in range(1, seqs)]
    chip_peers = [lax.rem(chip + d, chips) * CORES + core for d in range(1, chips)]

    barrier = pltpu.get_barrier_semaphore()
    for peer in seq_peers:
        pl.semaphore_signal(barrier, inc=1, device_id={"seq": peer}, device_id_type=MESH)
    for peer in chip_peers + [partner]:
        pl.semaphore_signal(barrier, inc=1, device_id={"chan": peer}, device_id_type=MESH)

    ins = []
    pairs = ((value_in, value), (gate1_in, gate1), (gate2_in, gate2), (filt1_in, filt1), (filt2_in, filt2), (segs_in, segs))
    for index, (source, target) in enumerate(pairs):
        copy = pltpu.make_async_copy(source, target, i_sem.at[index])
        copy.start()
        ins.append(copy)

    w_copies = []
    for side in range(CORES):
        owner = 1 - core if side == 0 else core
        for q in range(chunks):
            at = pl.multiple_of(owner * half_cols + q * width, width)
            copy = pltpu.make_async_copy(
                weight.at[:, pl.ds(at, width)], w_buf.at[side, q], w_sem.at[side, q]
            )
            copy.start()
            w_copies.append(copy)

    ins[0].wait()
    ins[1].wait()
    prod = (gate1[...].astype(jnp.float32) * value[...].astype(jnp.float32)).astype(jnp.bfloat16)
    z_send[...] = prod.T.reshape(seqs, rows, tok)

    pl.semaphore_wait(barrier, seqs - 1 + chips)

    def exchange(source, target, sends, recvs, part):
        span = pl.ds(part * part_rows, part_rows)
        started = []
        for d, peer in enumerate(seq_peers):
            copy = remote(
                source.at[peer, span], target.at[me, span], sends.at[part, d], recvs.at[part, d], {"seq": peer}
            )
            copy.start()
            started.append(copy)
        return started

    ins[5].wait()
    s_copies = []
    for d, peer in enumerate(seq_peers):
        copy = remote(segs, seg_all.at[me], s_ss.at[d], s_rs.at[d], {"seq": peer})
        copy.start()
        s_copies.append(copy)
    z_copies = [exchange(z_send, z_recv, z_ss, z_rs, 0)]
    ins[2].wait()
    g_send[...] = gate2[...].T.reshape(seqs, rows, tok)
    g_copies = [exchange(g_send, g_recv, g_ss, g_rs, 0)]
    for part in range(1, parts):
        z_copies.append(exchange(z_send, z_recv, z_ss, z_rs, part))
        g_copies.append(exchange(g_send, g_recv, g_ss, g_rs, part))
    seg_all[me] = segs[...]
    z_recv[me] = z_send[me]
    g_recv[me] = g_send[me]

    def build_taps(which, filt):
        taps_f32[which] = filt[...].astype(jnp.float32)

        def build(f, carry):
            row = taps_f32[which, pl.ds(me * mine_filts + f, 1), :]
            wide = jnp.broadcast_to(row, (LANES, length))
            low = pltpu.roll(wide, 0, 1, stride=1, stride_axis=0).astype(jnp.bfloat16)
            taps[which, f, pl.ds(0, LANES), :] = low
            taps[which, f, pl.ds(LANES, LANES), :] = jnp.concatenate(
                [low[:, length - LANES :], low[:, : length - LANES]], axis=1
            )
            return carry

        lax.fori_loop(0, mine_filts, build, 0)

    ins[3].wait()
    ins[4].wait()
    build_taps(0, filt1)

    for copy in s_copies:
        copy.wait_recv()

    ids = jnp.concatenate([seg_all[j] for j in range(seqs)], axis=1)
    first = jnp.broadcast_to((ids == 0).astype(jnp.float32), (per, length))
    in_first = first > 0.5
    keep = (first.astype(jnp.bfloat16), (1.0 - first).astype(jnp.bfloat16))

    def conv(which, f, field):
        parts = []
        for j in range(blocks):
            span = slice(j * TILE, (j + 1) * TILE)
            parts += [field[:, span] * keep[0][:, span], field[:, span] * keep[1][:, span]]
        lhs = jnp.concatenate(parts, axis=0)
        res = jnp.dot(lhs, taps[which, f], preferred_element_type=jnp.float32)
        sums = []
        for context in range(2):
            total = None
            for j in range(blocks):
                at = (2 * j + context) * per
                piece = res[at : at + per]
                if j:
                    cut = length - j * TILE
                    piece = jnp.concatenate([piece[:, cut:], piece[:, :cut]], axis=1)
                total = piece if total is None else total + piece
            sums.append(total)
        return jnp.where(in_first, sums[0], sums[1])

    def rows_of(f):
        return pl.ds(pl.multiple_of(f * per, per), per)

    def joined(ref, f):
        return jnp.concatenate([ref[j, rows_of(f), :] for j in range(seqs)], axis=1)

    def first_conv(base, i, carry):
        at = [base + i * step + k for k in range(step)]
        fields = [joined(z_recv, f) for f in at]
        results = [conv(0, f, field) for f, field in zip(at, fields)]
        for f, result in zip(at, results):
            mix[rows_of(f), :] = result
        return carry

    def second_conv(base, i, carry):
        at = [base + i * step + k for k in range(step)]
        fields = [(joined(g_recv, f).astype(jnp.float32) * mix[rows_of(f), :]).astype(jnp.bfloat16) for f in at]
        results = [conv(1, f, field).astype(jnp.bfloat16) for f, field in zip(at, fields)]
        for f, result in zip(at, results):
            for j in range(seqs):
                m_cols[j, rows_of(f), :] = result[:, j * tok : (j + 1) * tok]
        return carry

    sub = tok // HALVES
    m_copies = [[] for _ in range(HALVES)]

    def send_mixed(part, half):
        span = pl.ds(half * sub, sub)
        for d, peer in enumerate(seq_peers):
            copy = remote(
                m_send.at[part, peer, span], m_recv.at[part, me, span],
                m_ss.at[part, half, d], m_rs.at[part, half, d], {"seq": peer},
            )
            copy.start()
            m_copies[half].append(copy)

    for part in range(parts):
        base = part * part_filts
        for copy in z_copies[part]:
            copy.wait_recv()
        lax.fori_loop(0, part_filts // step, functools.partial(first_conv, base), 0)
        if part == 0:
            build_taps(1, filt2)
        for copy in g_copies[part]:
            copy.wait_recv()
        lax.fori_loop(0, part_filts // step, functools.partial(second_conv, base), 0)
        span = pl.ds(part * part_rows, part_rows)
        for j in range(seqs):
            m_send[part, j] = m_cols[j, span, :].T
        send_mixed(part, 0)
    for half in range(1, HALVES):
        for part in range(parts):
            send_mixed(part, half)
    for part in range(parts):
        m_recv[part, me] = m_send[part, me]
    for copy in w_copies:
        copy.wait()
    p_copies, x_copies, o_copies = [], [], []

    def others_columns(lhs, half, q):
        i = half * chunks + q
        p_send[i] = jnp.dot(lhs, w_buf[0, q], preferred_element_type=jnp.float32).astype(jnp.bfloat16)
        copy = remote(p_send.at[i], p_recv.at[i], p_ss.at[i], p_rs.at[i], {"chan": partner})
        copy.start()
        p_copies.append(copy)

    def my_columns(lhs, half, q):
        i = half * chunks + q
        part = jnp.dot(lhs, w_buf[1, q], preferred_element_type=jnp.float32)
        p_copies[i].wait_recv()
        x_buf[chip, i] = (part + p_recv[i].astype(jnp.float32)).astype(jnp.bfloat16)
        x_copies.append([])
        for d, peer in enumerate(chip_peers):
            copy = remote(x_buf.at[chip, i], x_buf.at[chip, i], x_ss.at[i, d], x_rs.at[i, d], {"chan": peer})
            copy.start()
            x_copies[i].append(copy)

    for half in range(HALVES):
        for copy in m_copies[half]:
            copy.wait_recv()
        span = slice(half * sub, (half + 1) * sub)
        lhs = jnp.concatenate(
            [m_recv[part, j, span, :] for j in range(seqs) for part in range(parts)], axis=1
        )
        others_columns(lhs, half, 0)
        for q in range(chunks):
            if q + 1 < chunks:
                others_columns(lhs, half, q + 1)
            my_columns(lhs, half, q)
    for half in range(HALVES):
        for q in range(chunks):
            i = half * chunks + q
            for copy in x_copies[i]:
                copy.wait_recv()
            total = x_buf[0, i].astype(jnp.float32)
            for j in range(1, chips):
                total = total + x_buf[j, i].astype(jnp.float32)
            cols = pl.ds(pl.multiple_of(core * half_cols + q * width, width), width)
            here = out.at[pl.ds(half * sub, sub), cols]
            here[...] = total.astype(jnp.bfloat16)
            copy = remote(here, here, o_ss.at[i], o_rs.at[i], {"chan": partner})
            copy.start()
            o_copies.append(copy)
    nested = [c for cs in z_copies + g_copies + m_copies + x_copies for c in cs]
    for copy in s_copies + nested + p_copies:
        copy.wait_send()
    for copy in o_copies:
        copy.wait()


def local(seqs, chans, value, gate1, gate2, filt1, filt2, weight, segs):
    tok, width = value.shape
    filts, length = filt1.shape
    cols = weight.shape[1]
    chips = chans // CORES
    chunks = 4
    chunk = cols // CORES // chunks
    mine = filts // seqs
    rows = width // seqs
    bf16, f32 = jnp.bfloat16, jnp.float32
    dma = pltpu.SemaphoreType.DMA
    others = seqs - 1
    pieces = HALVES * chunks
    parts = math.gcd(mine, PARTS)
    vmem = pl.BlockSpec(memory_space=pltpu.VMEM)
    return pl.pallas_call(
        functools.partial(kernel, seqs, chans, chunks),
        out_shape=jax.ShapeDtypeStruct((tok, cols), bf16),
        in_specs=[pl.BlockSpec(memory_space=pltpu.HBM)] * 7,
        out_specs=vmem,
        scratch_shapes=[
            pltpu.VMEM((tok, width), bf16),
            pltpu.VMEM((tok, width), bf16),
            pltpu.VMEM((tok, width), bf16),
            pltpu.VMEM((filts, length), bf16),
            pltpu.VMEM((filts, length), bf16),
            pltpu.VMEM((1, tok), jnp.int32),
            pltpu.VMEM((2, filts, length), f32),
            pltpu.VMEM((2, mine, TILE, length), bf16),
            pltpu.VMEM((seqs, rows, tok), bf16),
            pltpu.VMEM((seqs, rows, tok), bf16),
            pltpu.VMEM((seqs, rows, tok), bf16),
            pltpu.VMEM((seqs, rows, tok), bf16),
            pltpu.VMEM((seqs, 1, tok), jnp.int32),
            pltpu.VMEM((rows, length), f32),
            pltpu.VMEM((seqs, rows, tok), bf16),
            pltpu.VMEM((parts, seqs, tok, rows // parts), bf16),
            pltpu.VMEM((parts, seqs, tok, rows // parts), bf16),
            pltpu.VMEM((CORES, chunks, width, chunk), bf16),
            pltpu.VMEM((pieces, tok // HALVES, chunk), bf16),
            pltpu.VMEM((pieces, tok // HALVES, chunk), bf16),
            pltpu.VMEM((chips, pieces, tok // HALVES, chunk), bf16),
            dma((6,)),
            dma((CORES, chunks)),
            dma((parts, others)), dma((parts, others)), dma((parts, others)), dma((parts, others)),
            dma((others,)), dma((others,)), dma((parts, HALVES, others)), dma((parts, HALVES, others)),
            dma((pieces,)), dma((pieces,)),
            dma((pieces, chips - 1)), dma((pieces, chips - 1)),
            dma((pieces,)), dma((pieces,)),
        ],
        compiler_params=pltpu.CompilerParams(
            collective_id=0, has_side_effects=True, vmem_limit_bytes=58 * 1024 * 1024
        ),
    )(value, gate1, gate2, filt1, filt2, weight, segs.reshape(1, tok))


def solution(mesh):
    in_specs = (
        P(("groups", "seq"), "chan"),
        P(("groups", "seq"), "chan"),
        P(("groups", "seq"), "chan"),
        P("chan", None),
        P("chan", None),
        P("chan", None),
        P(("groups", "seq")),
    )
    out_specs = P(("groups", "seq"), None)
    body = functools.partial(local, mesh.shape["seq"], mesh.shape["chan"])
    return jax.shard_map(body, mesh=mesh, in_specs=in_specs, out_specs=out_specs, check_vma=False)
```

```python
import functools
import math

import jax
import jax.numpy as jnp
from jax import lax
from jax.experimental import pallas as pl
from jax.experimental.pallas import tpu as pltpu
from jax.sharding import PartitionSpec as P

MESH = pl.DeviceIdType.MESH
TILE = 256
LANES = 128
CORES = 2
GROUP = 4
PARTS = 2
HALVES = 2
STRIP = 16


def remote(src, dst, send, recv, where):
    return pltpu.make_async_remote_copy(
        src_ref=src, dst_ref=dst, send_sem=send, recv_sem=recv, device_id=where, device_id_type=MESH
    )


def kernel(
    seqs, chans, chunks,
    value_in, gate1_in, gate2_in, filt1_in, filt2_in, weight, segs_in,
    out,
    value, gate1, gate2, filt1, filt2, segs,
    taps_f32, taps, z_send, z_recv, g_send, g_recv, seg_all, mix, m_cols, m_send, m_recv,
    w_buf, p_send, p_recv, x_buf, o_buf,
    i_sem, w_sem, z_ss, z_rs, g_ss, g_rs, s_ss, s_rs, m_ss, m_rs, p_ss, p_rs, x_ss, x_rs, o_ss, o_rs, o_ls,
):
    me = lax.axis_index("seq")
    chan = lax.axis_index("chan")
    chips = chans // CORES
    core = lax.rem(chan, CORES)
    chip = lax.div(chan, CORES)
    partner = chip * CORES + (1 - core)
    tok = value.shape[0]
    length = filt1.shape[1]
    mine_filts = taps.shape[1]
    rows = z_send.shape[1]
    per = rows // mine_filts
    blocks = length // TILE
    parts = z_ss.shape[0]
    part_filts = mine_filts // parts
    part_rows = rows // parts
    step = math.gcd(part_filts, GROUP)
    half_cols = weight.shape[1] // CORES
    width = half_cols // chunks

    seq_peers = [lax.rem(me + d, seqs) for d in range(1, seqs)]
    chip_peers = [lax.rem(chip + d, chips) * CORES + core for d in range(1, chips)]

    barrier = pltpu.get_barrier_semaphore()
    for peer in seq_peers:
        pl.semaphore_signal(barrier, inc=1, device_id={"seq": peer}, device_id_type=MESH)
    for peer in chip_peers + [partner]:
        pl.semaphore_signal(barrier, inc=1, device_id={"chan": peer}, device_id_type=MESH)

    ins = []
    pairs = ((value_in, value), (gate1_in, gate1), (gate2_in, gate2), (filt1_in, filt1), (filt2_in, filt2), (segs_in, segs))
    for index, (source, target) in enumerate(pairs):
        copy = pltpu.make_async_copy(source, target, i_sem.at[index])
        copy.start()
        ins.append(copy)

    w_copies = []
    for side in range(CORES):
        owner = 1 - core if side == 0 else core
        for q in range(chunks):
            at = pl.multiple_of(owner * half_cols + q * width, width)
            copy = pltpu.make_async_copy(
                weight.at[:, pl.ds(at, width)], w_buf.at[side, q], w_sem.at[side, q]
            )
            copy.start()
            w_copies.append(copy)

    ins[0].wait()
    ins[1].wait()
    prod = (gate1[...].astype(jnp.float32) * value[...].astype(jnp.float32)).astype(jnp.bfloat16)
    z_send[...] = prod.T.reshape(seqs, rows, tok)

    pl.semaphore_wait(barrier, seqs - 1 + chips)

    def exchange(source, target, sends, recvs, part):
        span = pl.ds(part * part_rows, part_rows)
        started = []
        for d, peer in enumerate(seq_peers):
            copy = remote(
                source.at[peer, span], target.at[me, span], sends.at[part, d], recvs.at[part, d], {"seq": peer}
            )
            copy.start()
            started.append(copy)
        return started

    ins[5].wait()
    s_copies = []
    for d, peer in enumerate(seq_peers):
        copy = remote(segs, seg_all.at[me], s_ss.at[d], s_rs.at[d], {"seq": peer})
        copy.start()
        s_copies.append(copy)
    z_copies = [exchange(z_send, z_recv, z_ss, z_rs, 0)]
    ins[2].wait()
    g_send[...] = gate2[...].T.reshape(seqs, rows, tok)
    g_copies = [exchange(g_send, g_recv, g_ss, g_rs, 0)]
    for part in range(1, parts):
        z_copies.append(exchange(z_send, z_recv, z_ss, z_rs, part))
        g_copies.append(exchange(g_send, g_recv, g_ss, g_rs, part))
    seg_all[me] = segs[...]
    z_recv[me] = z_send[me]
    g_recv[me] = g_send[me]

    def build_taps(which, filt):
        taps_f32[which] = filt[...].astype(jnp.float32)

        def build(f, carry):
            row = taps_f32[which, pl.ds(me * mine_filts + f, 1), :]
            wide = jnp.broadcast_to(row, (LANES, length))
            low = pltpu.roll(wide, 0, 1, stride=1, stride_axis=0).astype(jnp.bfloat16)
            taps[which, f, pl.ds(0, LANES), :] = low
            taps[which, f, pl.ds(LANES, LANES), :] = jnp.concatenate(
                [low[:, length - LANES :], low[:, : length - LANES]], axis=1
            )
            return carry

        lax.fori_loop(0, mine_filts, build, 0)

    ins[3].wait()
    ins[4].wait()
    build_taps(0, filt1)

    for copy in s_copies:
        copy.wait_recv()

    ids = jnp.concatenate([seg_all[j] for j in range(seqs)], axis=1)
    first = jnp.broadcast_to((ids == 0).astype(jnp.float32), (per, length))
    in_first = first > 0.5
    keep = (first.astype(jnp.bfloat16), (1.0 - first).astype(jnp.bfloat16))

    def conv(which, f, field):
        parts = []
        for j in range(blocks):
            span = slice(j * TILE, (j + 1) * TILE)
            parts += [field[:, span] * keep[0][:, span], field[:, span] * keep[1][:, span]]
        lhs = jnp.concatenate(parts, axis=0)
        res = jnp.dot(lhs, taps[which, f], preferred_element_type=jnp.float32)
        sums = []
        for context in range(2):
            total = None
            for j in range(blocks):
                at = (2 * j + context) * per
                piece = res[at : at + per]
                if j:
                    cut = length - j * TILE
                    piece = jnp.concatenate([piece[:, cut:], piece[:, :cut]], axis=1)
                total = piece if total is None else total + piece
            sums.append(total)
        return jnp.where(in_first, sums[0], sums[1])

    def rows_of(f):
        return pl.ds(pl.multiple_of(f * per, per), per)

    def joined(ref, f):
        return jnp.concatenate([ref[j, rows_of(f), :] for j in range(seqs)], axis=1)

    def first_conv(base, i, carry):
        at = [base + i * step + k for k in range(step)]
        fields = [joined(z_recv, f) for f in at]
        results = [conv(0, f, field) for f, field in zip(at, fields)]
        for f, result in zip(at, results):
            mix[rows_of(f), :] = result
        return carry

    def second_conv(base, i, carry):
        at = [base + i * step + k for k in range(step)]
        fields = [(joined(g_recv, f).astype(jnp.float32) * mix[rows_of(f), :]).astype(jnp.bfloat16) for f in at]
        results = [conv(1, f, field).astype(jnp.bfloat16) for f, field in zip(at, fields)]
        for f, result in zip(at, results):
            for j in range(seqs):
                m_cols[j, rows_of(f), :] = result[:, j * tok : (j + 1) * tok]
        return carry

    sub = tok // HALVES
    m_copies = [[] for _ in range(HALVES)]

    def send_mixed(part, half):
        span = pl.ds(half * sub, sub)
        for d, peer in enumerate(seq_peers):
            copy = remote(
                m_send.at[part, peer, span], m_recv.at[part, me, span],
                m_ss.at[part, half, d], m_rs.at[part, half, d], {"seq": peer},
            )
            copy.start()
            m_copies[half].append(copy)

    for part in range(parts):
        base = part * part_filts
        for copy in z_copies[part]:
            copy.wait_recv()
        lax.fori_loop(0, part_filts // step, functools.partial(first_conv, base), 0)
        if part == 0:
            build_taps(1, filt2)
        for copy in g_copies[part]:
            copy.wait_recv()
        lax.fori_loop(0, part_filts // step, functools.partial(second_conv, base), 0)
        span = pl.ds(part * part_rows, part_rows)
        for j in range(seqs):
            m_send[part, j] = m_cols[j, span, :].T
        send_mixed(part, 0)
    for half in range(1, HALVES):
        for part in range(parts):
            send_mixed(part, half)
    for part in range(parts):
        m_recv[part, me] = m_send[part, me]
    for copy in w_copies:
        copy.wait()
    p_copies, x_copies, o_copies = [], [], []

    def others_columns(lhs, half, q):
        i = half * chunks + q
        p_send[i] = jnp.dot(lhs, w_buf[0, q], preferred_element_type=jnp.float32).astype(jnp.bfloat16)
        copy = remote(p_send.at[i], p_recv.at[i], p_ss.at[i], p_rs.at[i], {"chan": partner})
        copy.start()
        p_copies.append(copy)

    def my_columns(lhs, half, q):
        i = half * chunks + q
        part = jnp.dot(lhs, w_buf[1, q], preferred_element_type=jnp.float32)
        p_copies[i].wait_recv()
        x_buf[chip, i] = (part + p_recv[i].astype(jnp.float32)).astype(jnp.bfloat16)
        x_copies.append([])
        for d, peer in enumerate(chip_peers):
            copy = remote(x_buf.at[chip, i], x_buf.at[chip, i], x_ss.at[i, d], x_rs.at[i, d], {"chan": peer})
            copy.start()
            x_copies[i].append(copy)

    for half in range(HALVES):
        for copy in m_copies[half]:
            copy.wait_recv()
        span = slice(half * sub, (half + 1) * sub)
        lhs = jnp.concatenate(
            [m_recv[part, j, span, :] for j in range(seqs) for part in range(parts)], axis=1
        )
        others_columns(lhs, half, 0)
        for q in range(chunks):
            if q + 1 < chunks:
                others_columns(lhs, half, q + 1)
            my_columns(lhs, half, q)
    for half in range(HALVES):
        for q in range(chunks):
            i = half * chunks + q
            for copy in x_copies[i]:
                copy.wait_recv()
            total = x_buf[0, i].astype(jnp.float32)
            for j in range(1, chips):
                total = total + x_buf[j, i].astype(jnp.float32)
            cols = pl.ds(pl.multiple_of(core * half_cols + q * width, width), width)
            here = out.at[pl.ds(half * sub, sub), cols]
            o_buf[i] = total.astype(jnp.bfloat16)
            copy = pltpu.make_async_copy(o_buf.at[i], here, o_ls.at[i])
            copy.start()
            o_copies.append(copy)
            copy = remote(o_buf.at[i], here, o_ss.at[i], o_rs.at[i], {"chan": partner})
            copy.start()
            o_copies.append(copy)
    nested = [c for cs in z_copies + g_copies + m_copies + x_copies for c in cs]
    for copy in s_copies + nested + p_copies:
        copy.wait_send()
    for copy in o_copies:
        copy.wait()


def hand_on(source, target, sems):
    copies = []
    for i in range(source.shape[0] // STRIP):
        span = pl.ds(i * STRIP, STRIP)
        copy = pltpu.make_async_copy(source.at[span], target.at[span], sems.at[i])
        copy.start()
        copies.append(copy)
    for copy in copies:
        copy.wait()


def local(seqs, chans, value, gate1, gate2, filt1, filt2, weight, segs):
    tok, width = value.shape
    filts, length = filt1.shape
    cols = weight.shape[1]
    chips = chans // CORES
    chunks = 4
    chunk = cols // CORES // chunks
    mine = filts // seqs
    rows = width // seqs
    bf16, f32 = jnp.bfloat16, jnp.float32
    dma = pltpu.SemaphoreType.DMA
    others = seqs - 1
    pieces = HALVES * chunks
    parts = math.gcd(mine, PARTS)
    hbm = pl.BlockSpec(memory_space=pltpu.HBM)
    mixed = pl.pallas_call(
        functools.partial(kernel, seqs, chans, chunks),
        out_shape=jax.ShapeDtypeStruct((tok, cols), bf16),
        in_specs=[hbm] * 7,
        out_specs=hbm,
        scratch_shapes=[
            pltpu.VMEM((tok, width), bf16),
            pltpu.VMEM((tok, width), bf16),
            pltpu.VMEM((tok, width), bf16),
            pltpu.VMEM((filts, length), bf16),
            pltpu.VMEM((filts, length), bf16),
            pltpu.VMEM((1, tok), jnp.int32),
            pltpu.VMEM((2, filts, length), f32),
            pltpu.VMEM((2, mine, TILE, length), bf16),
            pltpu.VMEM((seqs, rows, tok), bf16),
            pltpu.VMEM((seqs, rows, tok), bf16),
            pltpu.VMEM((seqs, rows, tok), bf16),
            pltpu.VMEM((seqs, rows, tok), bf16),
            pltpu.VMEM((seqs, 1, tok), jnp.int32),
            pltpu.VMEM((rows, length), f32),
            pltpu.VMEM((seqs, rows, tok), bf16),
            pltpu.VMEM((parts, seqs, tok, rows // parts), bf16),
            pltpu.VMEM((parts, seqs, tok, rows // parts), bf16),
            pltpu.VMEM((CORES, chunks, width, chunk), bf16),
            pltpu.VMEM((pieces, tok // HALVES, chunk), bf16),
            pltpu.VMEM((pieces, tok // HALVES, chunk), bf16),
            pltpu.VMEM((chips, pieces, tok // HALVES, chunk), bf16),
            pltpu.VMEM((pieces, tok // HALVES, chunk), bf16),
            dma((6,)),
            dma((CORES, chunks)),
            dma((parts, others)), dma((parts, others)), dma((parts, others)), dma((parts, others)),
            dma((others,)), dma((others,)), dma((parts, HALVES, others)), dma((parts, HALVES, others)),
            dma((pieces,)), dma((pieces,)),
            dma((pieces, chips - 1)), dma((pieces, chips - 1)),
            dma((pieces,)), dma((pieces,)), dma((pieces,)),
        ],
        compiler_params=pltpu.CompilerParams(
            collective_id=0, has_side_effects=True, vmem_limit_bytes=58 * 1024 * 1024
        ),
    )(value, gate1, gate2, filt1, filt2, weight, segs.reshape(1, tok))
    return pl.pallas_call(
        hand_on,
        out_shape=jax.ShapeDtypeStruct((tok, cols), bf16),
        in_specs=[hbm],
        out_specs=hbm,
        scratch_shapes=[dma((tok // STRIP,))],
    )(mixed)


def solution(mesh):
    in_specs = (
        P(("groups", "seq"), "chan"),
        P(("groups", "seq"), "chan"),
        P(("groups", "seq"), "chan"),
        P("chan", None),
        P("chan", None),
        P("chan", None),
        P(("groups", "seq")),
    )
    out_specs = P(("groups", "seq"), None)
    body = functools.partial(local, mesh.shape["seq"], mesh.shape["chan"])
    return jax.shard_map(body, mesh=mesh, in_specs=in_specs, out_specs=out_specs, check_vma=False)
```

```python
import functools
import math

import jax
import jax.numpy as jnp
from jax import lax
from jax.experimental import pallas as pl
from jax.experimental.pallas import tpu as pltpu
from jax.sharding import PartitionSpec as P

MESH = pl.DeviceIdType.MESH
TILE = 256
LANES = 128
CORES = 2
GROUP = 4
PARTS = 2
HALVES = 2
STRIP = 16


def remote(src, dst, send, recv, where):
    return pltpu.make_async_remote_copy(
        src_ref=src, dst_ref=dst, send_sem=send, recv_sem=recv, device_id=where, device_id_type=MESH
    )


def kernel(
    seqs, chans, chunks,
    value_in, gate1_in, gate2_in, filt1_in, filt2_in, weight, segs_in,
    out,
    value, gate1, gate2, filt1, filt2, segs,
    taps_f32, taps, z_send, z_recv, g_send, g_recv, seg_all, mix, m_cols, m_send, m_recv,
    w_buf, p_send, p_recv, x_buf, o_buf,
    i_sem, w_sem, z_ss, z_rs, g_ss, g_rs, s_ss, s_rs, m_ss, m_rs, p_ss, p_rs, x_ss, x_rs, o_ss, o_rs, o_ls,
):
    me = lax.axis_index("seq")
    chan = lax.axis_index("chan")
    chips = chans // CORES
    core = lax.rem(chan, CORES)
    chip = lax.div(chan, CORES)
    partner = chip * CORES + (1 - core)
    tok = value.shape[0]
    length = filt1.shape[1]
    mine_filts = taps.shape[1]
    rows = z_send.shape[1]
    per = rows // mine_filts
    blocks = length // TILE
    parts = z_ss.shape[0]
    part_filts = mine_filts // parts
    part_rows = rows // parts
    step = math.gcd(part_filts, GROUP)
    half_cols = weight.shape[1] // CORES
    width = half_cols // chunks

    seq_peers = [lax.rem(me + d, seqs) for d in range(1, seqs)]
    chip_peers = [lax.rem(chip + d, chips) * CORES + core for d in range(1, chips)]

    barrier = pltpu.get_barrier_semaphore()
    for peer in seq_peers:
        pl.semaphore_signal(barrier, inc=1, device_id={"seq": peer}, device_id_type=MESH)
    for peer in chip_peers + [partner]:
        pl.semaphore_signal(barrier, inc=1, device_id={"chan": peer}, device_id_type=MESH)

    ins = []
    pairs = ((value_in, value), (gate1_in, gate1), (gate2_in, gate2), (filt1_in, filt1), (filt2_in, filt2), (segs_in, segs))
    for index, (source, target) in enumerate(pairs):
        copy = pltpu.make_async_copy(source, target, i_sem.at[index])
        copy.start()
        ins.append(copy)

    w_copies = []
    for side in range(CORES):
        owner = 1 - core if side == 0 else core
        for q in range(chunks):
            at = pl.multiple_of(owner * half_cols + q * width, width)
            copy = pltpu.make_async_copy(
                weight.at[:, pl.ds(at, width)], w_buf.at[side, q], w_sem.at[side, q]
            )
            copy.start()
            w_copies.append(copy)

    ins[0].wait()
    ins[1].wait()
    prod = (gate1[...].astype(jnp.float32) * value[...].astype(jnp.float32)).astype(jnp.bfloat16)
    z_send[...] = prod.T.reshape(seqs, rows, tok)

    pl.semaphore_wait(barrier, seqs - 1 + chips)

    def exchange(source, target, sends, recvs, part):
        span = pl.ds(part * part_rows, part_rows)
        started = []
        for d, peer in enumerate(seq_peers):
            copy = remote(
                source.at[peer, span], target.at[me, span], sends.at[part, d], recvs.at[part, d], {"seq": peer}
            )
            copy.start()
            started.append(copy)
        return started

    ins[5].wait()
    s_copies = []
    for d, peer in enumerate(seq_peers):
        copy = remote(segs, seg_all.at[me], s_ss.at[d], s_rs.at[d], {"seq": peer})
        copy.start()
        s_copies.append(copy)
    z_copies = [exchange(z_send, z_recv, z_ss, z_rs, 0)]
    ins[2].wait()
    g_send[...] = gate2[...].T.reshape(seqs, rows, tok)
    g_copies = [exchange(g_send, g_recv, g_ss, g_rs, 0)]
    for part in range(1, parts):
        z_copies.append(exchange(z_send, z_recv, z_ss, z_rs, part))
        g_copies.append(exchange(g_send, g_recv, g_ss, g_rs, part))
    seg_all[me] = segs[...]
    z_recv[me] = z_send[me]
    g_recv[me] = g_send[me]

    def build_taps(which, filt):
        taps_f32[which] = filt[...].astype(jnp.float32)

        def build(f, carry):
            row = taps_f32[which, pl.ds(me * mine_filts + f, 1), :]
            wide = jnp.broadcast_to(row, (LANES, length))
            low = pltpu.roll(wide, 0, 1, stride=1, stride_axis=0).astype(jnp.bfloat16)
            taps[which, f, pl.ds(0, LANES), :] = low
            taps[which, f, pl.ds(LANES, LANES), :] = jnp.concatenate(
                [low[:, length - LANES :], low[:, : length - LANES]], axis=1
            )
            return carry

        lax.fori_loop(0, mine_filts, build, 0)

    ins[3].wait()
    ins[4].wait()
    build_taps(0, filt1)

    for copy in s_copies:
        copy.wait_recv()

    ids = jnp.concatenate([seg_all[j] for j in range(seqs)], axis=1)
    first = jnp.broadcast_to((ids == 0).astype(jnp.float32), (per, length))
    in_first = first > 0.5
    keep = (first.astype(jnp.bfloat16), (1.0 - first).astype(jnp.bfloat16))

    def conv(which, f, field):
        parts = []
        for j in range(blocks):
            span = slice(j * TILE, (j + 1) * TILE)
            parts += [field[:, span] * keep[0][:, span], field[:, span] * keep[1][:, span]]
        lhs = jnp.concatenate(parts, axis=0)
        res = jnp.dot(lhs, taps[which, f], preferred_element_type=jnp.float32)
        sums = []
        for context in range(2):
            total = None
            for j in range(blocks):
                at = (2 * j + context) * per
                piece = res[at : at + per]
                if j:
                    cut = length - j * TILE
                    piece = jnp.concatenate([piece[:, cut:], piece[:, :cut]], axis=1)
                total = piece if total is None else total + piece
            sums.append(total)
        return jnp.where(in_first, sums[0], sums[1])

    def rows_of(f):
        return pl.ds(pl.multiple_of(f * per, per), per)

    def joined(ref, f):
        return jnp.concatenate([ref[j, rows_of(f), :] for j in range(seqs)], axis=1)

    def first_conv(base, i, carry):
        at = [base + i * step + k for k in range(step)]
        fields = [joined(z_recv, f) for f in at]
        results = [conv(0, f, field) for f, field in zip(at, fields)]
        for f, result in zip(at, results):
            mix[rows_of(f), :] = result
        return carry

    def second_conv(base, i, carry):
        at = [base + i * step + k for k in range(step)]
        fields = [(joined(g_recv, f).astype(jnp.float32) * mix[rows_of(f), :]).astype(jnp.bfloat16) for f in at]
        results = [conv(1, f, field).astype(jnp.bfloat16) for f, field in zip(at, fields)]
        for f, result in zip(at, results):
            for j in range(seqs):
                m_cols[j, rows_of(f), :] = result[:, j * tok : (j + 1) * tok]
        return carry

    sub = tok // HALVES
    m_copies = [[] for _ in range(HALVES)]

    def send_mixed(part, half):
        span = pl.ds(half * sub, sub)
        for d, peer in enumerate(seq_peers):
            copy = remote(
                m_send.at[part, peer, span], m_recv.at[part, me, span],
                m_ss.at[part, half, d], m_rs.at[part, half, d], {"seq": peer},
            )
            copy.start()
            m_copies[half].append(copy)

    for part in range(parts):
        base = part * part_filts
        for copy in z_copies[part]:
            copy.wait_recv()
        lax.fori_loop(0, part_filts // step, functools.partial(first_conv, base), 0)
        if part == 0:
            build_taps(1, filt2)
        for copy in g_copies[part]:
            copy.wait_recv()
        lax.fori_loop(0, part_filts // step, functools.partial(second_conv, base), 0)
        span = pl.ds(part * part_rows, part_rows)
        for j in range(seqs):
            m_send[part, j] = m_cols[j, span, :].T
        send_mixed(part, 0)
    for half in range(1, HALVES):
        for part in range(parts):
            send_mixed(part, half)
    for part in range(parts):
        m_recv[part, me] = m_send[part, me]
    for copy in w_copies:
        copy.wait()
    p_copies, x_copies, o_copies = [], [], []

    def others_columns(lhs, half, q):
        i = half * chunks + q
        p_send[i] = jnp.dot(lhs, w_buf[0, q], preferred_element_type=jnp.float32).astype(jnp.bfloat16)
        copy = remote(p_send.at[i], p_recv.at[i], p_ss.at[i], p_rs.at[i], {"chan": partner})
        copy.start()
        p_copies.append(copy)

    def my_columns(lhs, half, q):
        i = half * chunks + q
        part = jnp.dot(lhs, w_buf[1, q], preferred_element_type=jnp.float32)
        p_copies[i].wait_recv()
        x_buf[chip, i] = (part + p_recv[i].astype(jnp.float32)).astype(jnp.bfloat16)
        x_copies.append([])
        for d, peer in enumerate(chip_peers):
            copy = remote(x_buf.at[chip, i], x_buf.at[chip, i], x_ss.at[i, d], x_rs.at[i, d], {"chan": peer})
            copy.start()
            x_copies[i].append(copy)

    for half in range(HALVES):
        for copy in m_copies[half]:
            copy.wait_recv()
        span = slice(half * sub, (half + 1) * sub)
        lhs = jnp.concatenate(
            [m_recv[part, j, span, :] for j in range(seqs) for part in range(parts)], axis=1
        )
        others_columns(lhs, half, 0)
        for q in range(chunks):
            if q + 1 < chunks:
                others_columns(lhs, half, q + 1)
            my_columns(lhs, half, q)
    for half in range(HALVES):
        for q in range(chunks):
            i = half * chunks + q
            for copy in x_copies[i]:
                copy.wait_recv()
            total = x_buf[0, i].astype(jnp.float32)
            for j in range(1, chips):
                total = total + x_buf[j, i].astype(jnp.float32)
            cols = pl.ds(pl.multiple_of(core * half_cols + q * width, width), width)
            here = out.at[pl.ds(half * sub, sub), cols]
            o_buf[i] = total.astype(jnp.bfloat16)
            copy = pltpu.make_async_copy(o_buf.at[i], here, o_ls.at[i])
            copy.start()
            o_copies.append(copy)
            copy = remote(o_buf.at[i], here, o_ss.at[i], o_rs.at[i], {"chan": partner})
            copy.start()
            o_copies.append(copy)
    nested = [c for cs in z_copies + g_copies + m_copies + x_copies for c in cs]
    for copy in s_copies + nested + p_copies:
        copy.wait_send()
    for copy in o_copies:
        copy.wait()


def hand_on(source, target, held, in_sems, out_sems):
    arriving, leaving = [], []
    for i in range(source.shape[0] // STRIP):
        span = pl.ds(i * STRIP, STRIP)
        copy = pltpu.make_async_copy(source.at[span], held.at[span], in_sems.at[i])
        copy.start()
        arriving.append(copy)
    for i, copy in enumerate(arriving):
        span = pl.ds(i * STRIP, STRIP)
        copy.wait()
        copy = pltpu.make_async_copy(held.at[span], target.at[span], out_sems.at[i])
        copy.start()
        leaving.append(copy)
    for copy in leaving:
        copy.wait()


def local(seqs, chans, value, gate1, gate2, filt1, filt2, weight, segs):
    tok, width = value.shape
    filts, length = filt1.shape
    cols = weight.shape[1]
    chips = chans // CORES
    chunks = 4
    chunk = cols // CORES // chunks
    mine = filts // seqs
    rows = width // seqs
    bf16, f32 = jnp.bfloat16, jnp.float32
    dma = pltpu.SemaphoreType.DMA
    others = seqs - 1
    pieces = HALVES * chunks
    parts = math.gcd(mine, PARTS)
    hbm = pl.BlockSpec(memory_space=pltpu.HBM)
    mixed = pl.pallas_call(
        functools.partial(kernel, seqs, chans, chunks),
        out_shape=jax.ShapeDtypeStruct((tok, cols), bf16),
        in_specs=[hbm] * 7,
        out_specs=hbm,
        scratch_shapes=[
            pltpu.VMEM((tok, width), bf16),
            pltpu.VMEM((tok, width), bf16),
            pltpu.VMEM((tok, width), bf16),
            pltpu.VMEM((filts, length), bf16),
            pltpu.VMEM((filts, length), bf16),
            pltpu.VMEM((1, tok), jnp.int32),
            pltpu.VMEM((2, filts, length), f32),
            pltpu.VMEM((2, mine, TILE, length), bf16),
            pltpu.VMEM((seqs, rows, tok), bf16),
            pltpu.VMEM((seqs, rows, tok), bf16),
            pltpu.VMEM((seqs, rows, tok), bf16),
            pltpu.VMEM((seqs, rows, tok), bf16),
            pltpu.VMEM((seqs, 1, tok), jnp.int32),
            pltpu.VMEM((rows, length), f32),
            pltpu.VMEM((seqs, rows, tok), bf16),
            pltpu.VMEM((parts, seqs, tok, rows // parts), bf16),
            pltpu.VMEM((parts, seqs, tok, rows // parts), bf16),
            pltpu.VMEM((CORES, chunks, width, chunk), bf16),
            pltpu.VMEM((pieces, tok // HALVES, chunk), bf16),
            pltpu.VMEM((pieces, tok // HALVES, chunk), bf16),
            pltpu.VMEM((chips, pieces, tok // HALVES, chunk), bf16),
            pltpu.VMEM((pieces, tok // HALVES, chunk), bf16),
            dma((6,)),
            dma((CORES, chunks)),
            dma((parts, others)), dma((parts, others)), dma((parts, others)), dma((parts, others)),
            dma((others,)), dma((others,)), dma((parts, HALVES, others)), dma((parts, HALVES, others)),
            dma((pieces,)), dma((pieces,)),
            dma((pieces, chips - 1)), dma((pieces, chips - 1)),
            dma((pieces,)), dma((pieces,)), dma((pieces,)),
        ],
        compiler_params=pltpu.CompilerParams(
            collective_id=0, has_side_effects=True, vmem_limit_bytes=58 * 1024 * 1024
        ),
    )(value, gate1, gate2, filt1, filt2, weight, segs.reshape(1, tok))
    return pl.pallas_call(
        hand_on,
        out_shape=jax.ShapeDtypeStruct((tok, cols), bf16),
        in_specs=[hbm],
        out_specs=hbm,
        scratch_shapes=[pltpu.VMEM((tok, cols), bf16), dma((tok // STRIP,)), dma((tok // STRIP,))],
    )(mixed)


def solution(mesh):
    in_specs = (
        P(("groups", "seq"), "chan"),
        P(("groups", "seq"), "chan"),
        P(("groups", "seq"), "chan"),
        P("chan", None),
        P("chan", None),
        P("chan", None),
        P(("groups", "seq")),
    )
    out_specs = P(("groups", "seq"), None)
    body = functools.partial(local, mesh.shape["seq"], mesh.shape["chan"])
    return jax.shard_map(body, mesh=mesh, in_specs=in_specs, out_specs=out_specs, check_vma=False)
```
